32 devices in a mesh: groups: 2 (over x), rows: 8 (over z, y), cols: 2 (over core).
Axes of the slice: x: 2, y: 2, z: 4, core: 2. Of those that a mesh axis runs over, the one named last changes fastest.
Arguments:
- train_emb: bfloat16 [32768, 768], P(('groups', 'rows')), parts along dimension 0
- val_emb: bfloat16 [4, 2048, 768], P(('groups', 'cols')), parts along dimension 0
- tiles: int32 [64, 2, 2], P(('groups', 'rows'), 'cols'), parts along dimension 0, may hold values from 0 to 3, as said below
- counts: int32 [64], P(('groups', 'rows')), parts along dimension 0, may hold values from 1 to 512, 12288 in all
Outputs:
- pot_train: float32 [32768], P(('groups', 'rows')), parts along dimension 0
- pot_val: float32 [4, 2048], P(('groups', 'cols')), parts along dimension 0
- grad_train: bfloat16 [32768, 768], P(('groups', 'rows'), 'cols'), parts along dimension 0
- grad_val: float32 [4, 2048, 768], P(('groups', 'cols'), 'rows'), parts along dimension 0
The draws below stay inside these ranges and needn't reach their ends.
There are 2 independent parts, one for each index of `groups`. The reference program is written for one: setup_inputs(seed, part) draws one part's arguments, and reference() takes and returns one part's arrays. A program takes and returns all parts, laid end to end along the dimension named above; each array names one. Nothing has to cross between parts.
Inputs may be any that keep to these rules, and one draw needn't show every extreme that they name: `tiles`: local validation block index within the column half; the 2 entries of one training block and half differ, and every validation block is paired with some training block in every draw. The counts sum to 12288; some block is full.
All inputs are finite; a program needn't handle non-finite values.
Results may differ from the reference program's by a relative error of at most 0.0029.
Values sent between devices are 32-bit elements; how exact they have to be, the bound alone decides.
A program may use at most 128 MiB of HBM per device.

```python
import math
import jax
import jax.numpy as jnp
import numpy as np
from jax import lax

D = 768
BLOCK = 512
TPC = 2
ITERS = 3
VB_COL = 4
NTB = 32
NTR = 16384
VAL_COL = 2048
NVA = 4096
LIVE = 12288
N_COLS = 2


def embed_rows(key, count, top_scale):
    first, second = jax.random.split(key, 2)
    scales = jnp.exp(jax.random.uniform(first, (count, 1), jnp.float32, 0.0, math.log(top_scale)))
    entries = jax.random.normal(second, (count, D), jnp.float32)
    return entries * scales / math.sqrt(D)


def draw_train_emb(key, part):
    key = jax.random.fold_in(key, 11)
    values = embed_rows(key, NTR, 3.0)
    return values.astype(jnp.bfloat16)


def draw_val_emb(key, part):
    key = jax.random.fold_in(key, 23)
    values = embed_rows(key, NVA, 3.0)
    return values.reshape(N_COLS, VAL_COL, D).astype(jnp.bfloat16)


def draw_tiles(key, part):
    key = jax.random.fold_in(key, 37)
    first, second = jax.random.split(key)
    shifts = jax.random.randint(first, (1, N_COLS), 0, VB_COL)
    base_block = (jnp.arange(NTB, dtype=jnp.int32)[:, None] + shifts) % VB_COL
    row_keys = jax.random.split(second, NTB * N_COLS)
    orders = jax.vmap(lambda one_key: jax.random.permutation(one_key, VB_COL))(row_keys).reshape(NTB, N_COLS, VB_COL)
    marked = (jnp.arange(VB_COL, dtype=jnp.int32)[None, None, :] == base_block[:, :, None]).astype(jnp.int32)
    ranking = orders.astype(jnp.int32) + VB_COL * marked
    chosen_values, chosen_index = jax.lax.top_k(ranking, TPC)
    return chosen_index.astype(jnp.int32)


def length_profile(count, total, limit, lean):
    loads = [(1 << 20) // math.isqrt(standing ** lean) + 1 for standing in range(2, count + 1)]
    surplus, given = total - limit - (count - 1), [1] * (count - 1)
    while surplus > 0:
        movable = [i for i in range(count - 1) if given[i] < limit]
        mass, budget = sum([loads[i] for i in movable]), surplus
        for i in movable:
            extra = min(limit - given[i], max(1, budget * loads[i] // mass), surplus)
            given[i] = given[i] + extra
            surplus = surplus - extra
    return np.array([limit] + given)


def ragged(own_key, amount, total, bound, lean):
    if amount == 2:
        one = jax.random.randint(own_key, (), max(1, total - bound), min(bound, total - 1) + 1)
        return jnp.stack([one, total - one])
    tallies = jnp.asarray(length_profile(amount, total, bound, lean), jnp.int32)
    pairs = (amount - 1) // 2
    donor, receiver = tallies[1:1 + 2 * pairs:2], tallies[2:2 + 2 * pairs:2]
    margin = jnp.minimum(donor - 1, bound - receiver)
    passed = jax.random.randint(jax.random.fold_in(own_key, 1), (pairs,), 0, 1 << 20) % (margin + 1)
    tallies = tallies.at[1:1 + 2 * pairs:2].set(donor - passed).at[2:2 + 2 * pairs:2].set(receiver + passed)
    return tallies[jax.random.permutation(jax.random.fold_in(own_key, 2), amount)]


def setup_inputs(seed: int = 0, part: int = 0) -> dict:
    key_of = jax.random.split(jax.random.key(seed), 5)
    part_splits = jax.random.split(jax.random.fold_in(key_of[4], part), 5)
    train_emb = draw_train_emb(jax.random.fold_in(jax.random.fold_in(key_of[4], part), 71), part)
    val_emb = draw_val_emb(jax.random.fold_in(jax.random.fold_in(key_of[4], part), 71), part)
    tiles = draw_tiles(jax.random.fold_in(jax.random.fold_in(key_of[4], part), 71), part)
    counts = ragged(part_splits[3], NTB, LIVE, BLOCK, 2).astype(jnp.int32)
    return {"train_emb": train_emb, "val_emb": val_emb, "tiles": tiles, "counts": counts}


entropy_weight = 0.1
floor_value = -1.0e30


def reference(train_emb, val_emb, tiles, counts):
    train_rows = train_emb.reshape(NTB, BLOCK, D)
    val_blocks = val_emb.reshape(N_COLS, VB_COL, BLOCK, D)
    live_rows = jnp.arange(BLOCK, dtype=jnp.int32)[None, :] < counts[:, None]
    live_mask = live_rows[:, None, None, :, None]
    train_sq = jnp.sum(jnp.square(train_rows.astype(jnp.float32)), axis=-1)
    val_sq = jnp.sum(jnp.square(val_blocks.astype(jnp.float32)), axis=-1)
    column_ids = jnp.arange(N_COLS, dtype=jnp.int32)[None, :, None]
    half_ids = jnp.arange(N_COLS, dtype=jnp.int32)[:, None]

    def tile_dots(inputs):
        block_rows, picked = inputs
        chosen = val_blocks[half_ids, picked].astype(jnp.float32)
        return jnp.einsum("id,ckjd->ckij", block_rows.astype(jnp.float32), chosen)

    inner_prod = lax.map(tile_dots, (train_rows, tiles))
    cost_tiles = train_sq[:, None, None, :, None] + val_sq[column_ids, tiles][:, :, :, None, :] - 2.0 * inner_prod
    block_hot = (tiles[..., None] == jnp.arange(VB_COL, dtype=jnp.int32)).astype(jnp.float32)
    pot_val = jnp.zeros((N_COLS, VB_COL, BLOCK), jnp.float32)
    pot_train = jnp.zeros((NTB, BLOCK), jnp.float32)
    for sweep_index in range(ITERS):
        val_near = pot_val[column_ids, tiles]
        scores = (val_near[:, :, :, None, :] - cost_tiles) / entropy_weight
        row_top = jnp.max(scores, axis=(1, 2, 4))
        row_total = jnp.sum(jnp.exp(scores - row_top[:, None, None, :, None]), axis=(1, 2, 4))
        pot_train = jnp.where(live_rows, -entropy_weight * (row_top + jnp.log(row_total)) + entropy_weight * jnp.log(1.0 / LIVE), 0.0)
        back_scores = jnp.where(live_mask, (pot_train[:, None, None, :, None] - cost_tiles) / entropy_weight, floor_value)
        tile_top = jnp.max(back_scores, axis=3)
        val_top = jnp.max(jnp.where(block_hot[..., None] > 0, tile_top[:, :, :, None, :], floor_value), axis=(0, 2))
        tile_sum = jnp.sum(jnp.exp(back_scores - val_top[column_ids, tiles][:, :, :, None, :]), axis=3)
        val_sum = jnp.einsum("tckv,tckj->cvj", block_hot, tile_sum, precision=lax.Precision.HIGHEST)
        pot_val = -entropy_weight * (val_top + jnp.log(val_sum)) + entropy_weight * jnp.log(1.0 / NVA)
    val_near = pot_val[column_ids, tiles]
    transport = jnp.where(live_mask, jnp.exp((pot_train[:, None, None, :, None] + val_near[:, :, :, None, :] - cost_tiles) / entropy_weight), 0.0)
    row_mass = jnp.sum(transport, axis=(1, 2, 4))
    plan_rounded = transport.astype(jnp.bfloat16)

    def per_block(carry_sum, scanned):
        weights, picked, block_rows, block_flags = scanned
        chosen = val_blocks[half_ids, picked].astype(jnp.float32)
        plan_float = weights.astype(jnp.float32)
        pulled = jnp.einsum("ckij,ckjd->id", plan_float, chosen)
        pushed = jnp.einsum("ckij,id->ckjd", plan_float, block_rows.astype(jnp.float32))
        carry_sum = carry_sum + jnp.einsum("ckv,ckjd->cvjd", block_flags, pushed, precision=lax.Precision.HIGHEST)
        return carry_sum, pulled

    start_sum = jnp.zeros((N_COLS, VB_COL, BLOCK, D), jnp.float32)
    pushed_sum, pulled_all = lax.scan(per_block, start_sum, (plan_rounded, tiles, train_rows, block_hot))
    grad_train = (LIVE * 2.0 * (row_mass[..., None] * train_rows.astype(jnp.float32) - pulled_all)).astype(jnp.bfloat16).reshape(NTR, D)
    grad_val = (2.0 * (val_blocks.astype(jnp.float32) - NVA * pushed_sum)).reshape(N_COLS, VAL_COL, D)
    return pot_train.reshape(NTR), pot_val.reshape(N_COLS, VAL_COL), grad_train, grad_val
```

```python
import functools
import math

import jax
import jax.numpy as jnp
from jax import lax
from jax.experimental import pallas as pl
from jax.experimental.pallas import tpu as pltpu
from jax.sharding import PartitionSpec as P

BLOCK = 512
ITERS = 3
LANES = 128
WEIGHT = 0.1
SCALE = math.log2(math.e) / WEIGHT
FLOOR = -1e30
MESH = pl.DeviceIdType.MESH
STRIPS = BLOCK // LANES


def strip(index):
    return pl.ds(index * LANES, LANES)


def diagonal():
    return lax.broadcasted_iota(jnp.int32, (LANES, LANES), 0) == lax.broadcasted_iota(
        jnp.int32, (LANES, LANES), 1
    )


def to_row(column):
    return jnp.sum(
        jnp.where(diagonal(), jnp.broadcast_to(column, (LANES, LANES)), 0.0), axis=0, keepdims=True
    )


def to_column(row):
    return jnp.sum(
        jnp.where(diagonal(), jnp.broadcast_to(row, (LANES, LANES)), 0.0), axis=1, keepdims=True
    )


def kernel(
    n, blocks, vals,
    tiles_ref, counts_ref, x_ref, y_ref,
    pot_train_ref, pot_val_ref, grad_train_ref, grad_val_ref,
    cost, plan, chosen, val_sq, g_ref, f_wide, mass_wide, tile_top, tile_sum, row_part,
    row_box, val_box, away, home, paired, landed, term_out, term_in,
    row_send, row_recv, val_send, val_recv, pair_send, pair_recv, own_send, own_recv,
    term_send, term_recv,
):
    me = lax.axis_index("rows")
    core = lax.axis_index("cols")
    other = 1 - core
    width = x_ref.shape[1]
    half_width = width // 2
    live_total = blocks * n * (3 * BLOCK // 4)
    val_total = vals * BLOCK * 2
    pairs = n // 2
    share = vals * BLOCK // n
    stage = lax.div(me, 2)
    side = lax.rem(me, 2)
    mate = stage * 2 + 1 - side

    barrier = pltpu.get_barrier_semaphore()

    @pl.loop(1, n)
    def _(d):
        pl.semaphore_signal(
            barrier, inc=1, device_id={"rows": lax.rem(me + d, n)}, device_id_type=MESH
        )

    pl.semaphore_signal(barrier, inc=1, device_id={"cols": other}, device_id_type=MESH)
    pl.semaphore_wait(barrier, n)

    def pick(q, rows_of, spare):
        found = rows_of(0)
        for v in range(1, vals):
            found = jnp.where(tiles_ref[q][:, 0:spare] == v, rows_of(v), found)
        return found

    def g_of(q):
        return pick(q, lambda v: g_ref[v], BLOCK)

    def block_rows(index):
        return pl.ds(pl.multiple_of(index * BLOCK, BLOCK), BLOCK)

    for v in range(vals):
        for c in range(STRIPS):
            rows = y_ref[pl.ds(v * BLOCK + c * LANES, LANES), :].astype(jnp.float32)
            val_sq[v, :, strip(c)] = to_row(jnp.sum(rows * rows, axis=1, keepdims=True))

    @pl.loop(0, blocks)
    def _(t):
        x = x_ref[block_rows(t), :]
        xf = x.astype(jnp.float32)
        x_sq = jnp.sum(xf * xf, axis=1, keepdims=True)
        for k in range(2):
            q = t * 2 + k
            for j in range(width // LANES):
                chosen[q, :, strip(j)] = pick(
                    q, lambda v: y_ref[v * BLOCK : (v + 1) * BLOCK, strip(j)], LANES
                )
            inner = lax.dot_general(
                x, chosen[q], (((1,), (1,)), ((), ())),
                preferred_element_type=jnp.float32,
            )
            cost[t * 2 + k] = ((x_sq + pick(q, lambda v: val_sq[v], BLOCK)) - 2.0 * inner) * SCALE

    g_ref[...] = jnp.zeros_like(g_ref)

    def val_copy(it, peer, slot):
        return pltpu.make_async_remote_copy(
            src_ref=val_box.at[it, slot], dst_ref=val_box.at[it, slot],
            send_sem=val_send.at[it, peer], recv_sem=val_recv.at[it, slot],
            device_id={"rows": peer}, device_id_type=MESH,
        )

    @pl.loop(0, ITERS)
    def _(it):
        @pl.loop(0, blocks)
        def _(t):
            g = [g_of(t * 2 + k) for k in range(2)]
            for c in range(STRIPS):
                def score(k, j):
                    return g[k][:, j * LANES : (j + 1) * LANES] - cost[t * 2 + k, strip(c), strip(j)]
                top = jnp.full((LANES, LANES), FLOOR, jnp.float32)
                for k in range(2):
                    for j in range(STRIPS):
                        top = jnp.maximum(top, score(k, j))
                top = jnp.max(top, axis=1, keepdims=True)
                wide = jnp.broadcast_to(top, (LANES, LANES))
                total = jnp.zeros((LANES, LANES), jnp.float32)
                for k in range(2):
                    for j in range(STRIPS):
                        total = total + jnp.exp2(score(k, j) - wide)
                total = jnp.sum(total, axis=1, keepdims=True)
                row_part[t, :, strip(c)] = to_row(top)
                row_part[blocks + t, :, strip(c)] = to_row(total)

        for q in range(2 * blocks):
            row_box[it, core, q : q + 1, :] = row_part[q]
        out = pltpu.make_async_remote_copy(
            src_ref=row_box.at[it, core], dst_ref=row_box.at[it, core],
            send_sem=row_send.at[it], recv_sem=row_recv.at[it],
            device_id={"cols": other}, device_id_type=MESH,
        )
        out.start()
        out.wait()
        tops = [row_box[it, q, 0:blocks, :] for q in range(2)]
        top = jnp.maximum(tops[0], tops[1])
        total = sum(
            row_box[it, q, blocks : 2 * blocks, :] * jnp.exp2(tops[q] - top) for q in range(2)
        )
        f_all = math.log2(1.0 / live_total) - (top + jnp.log2(total))
        lane = lax.broadcasted_iota(jnp.int32, (1, BLOCK), 1)
        for t in range(blocks):
            live = lane < counts_ref[t]
            pot_train_ref[t : t + 1, :] = jnp.where(live, f_all[t : t + 1] * (1.0 / SCALE), 0.0)
            f = jnp.where(live, f_all[t : t + 1], FLOOR)
            for c in range(STRIPS):
                f_wide[pl.ds(t * BLOCK + c * LANES, LANES), :] = jnp.broadcast_to(
                    to_column(f[:, c * LANES : (c + 1) * LANES]), (LANES, LANES)
                )

        @pl.loop(0, blocks)
        def _(t):
            for k in range(2):
                for c in range(STRIPS):
                    score = f_wide[block_rows(t), :] - cost[t * 2 + k, :, strip(c)]
                    top = jnp.max(score, axis=0, keepdims=True)
                    total = jnp.sum(jnp.exp2(score - top), axis=0, keepdims=True)
                    tile_top[t * 2 + k, :, strip(c)] = top
                    tile_sum[t * 2 + k, :, strip(c)] = total

        for v in range(vals):
            top = jnp.full((1, BLOCK), FLOOR, jnp.float32)
            for q in range(2 * blocks):
                top = jnp.maximum(top, jnp.where(tiles_ref[q] == v, tile_top[q], FLOOR))
            total = jnp.zeros((1, BLOCK), jnp.float32)
            for q in range(2 * blocks):
                scaled = tile_sum[q] * jnp.exp2(jnp.minimum(tile_top[q] - top, 0.0))
                total = total + jnp.where(tiles_ref[q] == v, scaled, 0.0)
            val_box[it, me, v : v + 1, :] = top
            val_box[it, me, vals + v : vals + v + 1, :] = total

        @pl.loop(1, n)
        def _(d):
            val_copy(it, lax.rem(me + d, n), me).start()

        @pl.loop(1, n)
        def _(d):
            val_copy(it, lax.rem(me + d, n), lax.rem(me + d, n)).wait_recv()

        top = val_box[it, 0, 0:vals, :]
        for q in range(1, n):
            top = jnp.maximum(top, val_box[it, q, 0:vals, :])
        total = jnp.zeros((vals, BLOCK), jnp.float32)
        for q in range(n):
            total = total + val_box[it, q, vals : 2 * vals, :] * jnp.exp2(val_box[it, q, 0:vals, :] - top)
        g = math.log2(1.0 / val_total) - (top + jnp.log2(total))
        pot_val_ref[...] = g * (1.0 / SCALE)
        for v in range(vals):
            g_ref[v] = g[v : v + 1]

    @pl.loop(0, blocks)
    def _(t):
        g = [g_of(t * 2 + k) for k in range(2)]
        for c in range(STRIPS):
            f = f_wide[pl.ds(pl.multiple_of(t * BLOCK + c * LANES, LANES), LANES), :]
            total = jnp.zeros((LANES, LANES), jnp.float32)
            for k in range(2):
                for j in range(STRIPS):
                    value = jnp.exp2(
                        f + g[k][:, j * LANES : (j + 1) * LANES] - cost[t * 2 + k, strip(c), strip(j)]
                    )
                    total = total + value
                    plan[t * 2 + k, strip(c), strip(j)] = value.astype(jnp.bfloat16)
            mass_wide[pl.ds(pl.multiple_of(t * BLOCK + c * LANES, LANES), LANES), :] = (
                jnp.broadcast_to(jnp.sum(total, axis=1, keepdims=True), (LANES, LANES))
            )

    def pair_copy(s):
        return pltpu.make_async_remote_copy(
            src_ref=away.at[s], dst_ref=paired.at[s],
            send_sem=pair_send.at[s], recv_sem=pair_recv.at[s],
            device_id={"rows": mate}, device_id_type=MESH,
        )

    def own_copy(s, slot):
        goal = lax.rem(stage + 1 + s, pairs)
        return pltpu.make_async_remote_copy(
            src_ref=home.at[s], dst_ref=landed.at[slot],
            send_sem=own_send.at[s], recv_sem=own_recv.at[slot],
            device_id={"rows": goal * 2 + side}, device_id_type=MESH,
        )

    def term_copy(t):
        return pltpu.make_async_remote_copy(
            src_ref=term_out.at[t], dst_ref=term_in.at[t],
            send_sem=term_send.at[t], recv_sem=term_recv.at[t],
            device_id={"cols": other}, device_id_type=MESH,
        )

    @pl.loop(0, pairs)
    def _(s):
        goal = lax.rem(stage + 1 + s, pairs)

        def push(which):
            start = (goal * 2 + which) * share
            v = lax.div(start, BLOCK)
            inside = lax.rem(start, BLOCK)
            total = jnp.zeros((share, width), jnp.float32)
            for t in range(blocks):
                if share % LANES == 0:
                    span = pl.ds(pl.multiple_of(inside, share), share)
                    parts = [plan[t * 2 + k, :, span] for k in range(2)]
                    offset = None
                else:
                    base = lax.div(inside, LANES) * LANES
                    span = pl.ds(pl.multiple_of(base, LANES), LANES)
                    parts = [plan[t * 2 + k, :, span] for k in range(2)]
                    offset = inside - base
                zero = jnp.zeros_like(parts[0])
                picked = jnp.where(
                    tiles_ref[t * 2][:, 0 : zero.shape[1]] == v, parts[0],
                    jnp.where(tiles_ref[t * 2 + 1][:, 0 : zero.shape[1]] == v, parts[1], zero),
                )
                product = lax.dot_general(
                    picked, x_ref[t * BLOCK : (t + 1) * BLOCK, :], (((0,), (0,)), ((), ())),
                    preferred_element_type=jnp.float32,
                )
                if offset is not None:
                    keep = product[0:share]
                    for piece in range(1, LANES // share):
                        keep = jnp.where(
                            offset == piece * share, product[piece * share : (piece + 1) * share], keep
                        )
                    product = keep
                total = total + product
            return total

        away[s] = push(1 - side)
        pair_copy(s).start()
        home[s] = push(side)

    @pl.loop(0, blocks)
    def _(t):
        mass = mass_wide[block_rows(t), 0:1]

        def pull(which):
            span = pl.ds(pl.multiple_of(which * half_width, LANES), half_width)
            total = mass * x_ref[block_rows(t), span].astype(jnp.float32)
            pulled = sum(
                jnp.dot(
                    plan[t * 2 + k], chosen[t * 2 + k, :, span],
                    preferred_element_type=jnp.float32,
                )
                for k in range(2)
            )
            return total - pulled

        term_out[t] = pull(other)
        term_copy(t).start()
        cost[t, :, 0:half_width] = pull(core)

    @pl.loop(0, blocks)
    def _(t):
        term_copy(t).wait()
        grad_train_ref[block_rows(t), :] = (
            live_total * 2.0 * (cost[t, :, 0:half_width] + term_in[t])
        ).astype(jnp.bfloat16)

    @pl.loop(0, pairs - 1)
    def _(s):
        pair_copy(s).wait_recv()
        home[s] = home[s] + paired[s]
        own_copy(s, stage).start()

    pair_copy(pairs - 1).wait_recv()
    home[pairs - 1] = home[pairs - 1] + paired[pairs - 1]

    @pl.loop(0, pairs - 1)
    def _(s):
        slot = lax.rem(stage + 1 + s, pairs)
        own_copy(s, slot).wait_recv()
        home[pairs - 1] = home[pairs - 1] + landed[slot]

    own_rows = y_ref[pl.ds(pl.multiple_of(me * share, share), share), :].astype(jnp.float32)
    grad_val_ref[...] = 2.0 * (own_rows - val_total * home[pairs - 1])

    @pl.loop(0, pairs)
    def _(s):
        pair_copy(s).wait_send()

    @pl.loop(0, pairs - 1)
    def _(s):
        own_copy(s, stage).wait_send()

    @pl.loop(0, ITERS)
    def _(it):
        @pl.loop(1, n)
        def _(d):
            val_copy(it, lax.rem(me + d, n), me).wait_send()


def body(train_emb, val_emb, tiles, counts):
    n = lax.axis_size("rows")
    rows, width = train_emb.shape
    blocks = counts.shape[0]
    val_rows = val_emb.shape[1]
    vals = val_rows // BLOCK
    share = val_rows // n
    pairs = n // 2
    half = width // 2
    f32, bf16 = jnp.float32, jnp.bfloat16
    dma = pltpu.SemaphoreType.DMA
    vmem = pl.BlockSpec(memory_space=pltpu.VMEM)
    pot_train, pot_val, grad_train, grad_val = pl.pallas_call(
        functools.partial(kernel, n, blocks, vals),
        out_shape=(
            jax.ShapeDtypeStruct((blocks, BLOCK), f32),
            jax.ShapeDtypeStruct((vals, BLOCK), f32),
            jax.ShapeDtypeStruct((rows, half), bf16),
            jax.ShapeDtypeStruct((share, width), f32),
        ),
        in_specs=[vmem, vmem, vmem, vmem],
        out_specs=(vmem, vmem, vmem, vmem),
        scratch_shapes=[
            pltpu.VMEM((2 * blocks, BLOCK, BLOCK), f32),
            pltpu.VMEM((2 * blocks, BLOCK, BLOCK), bf16),
            pltpu.VMEM((2 * blocks, BLOCK, width), bf16),
            pltpu.VMEM((vals, 1, BLOCK), f32),
            pltpu.VMEM((vals, 1, BLOCK), f32),
            pltpu.VMEM((rows, LANES), f32),
            pltpu.VMEM((rows, LANES), f32),
            pltpu.VMEM((2 * blocks, 1, BLOCK), f32),
            pltpu.VMEM((2 * blocks, 1, BLOCK), f32),
            pltpu.VMEM((2 * blocks, 1, BLOCK), f32),
            pltpu.VMEM((ITERS, 2, 2 * blocks, BLOCK), f32),
            pltpu.VMEM((ITERS, n, 2 * vals, BLOCK), f32),
            pltpu.VMEM((pairs, share, width), f32),
            pltpu.VMEM((pairs, share, width), f32),
            pltpu.VMEM((pairs, share, width), f32),
            pltpu.VMEM((pairs, share, width), f32),
            pltpu.VMEM((blocks, BLOCK, half), f32),
            pltpu.VMEM((blocks, BLOCK, half), f32),
            dma((ITERS,)), dma((ITERS,)),
            dma((ITERS, n)), dma((ITERS, n)),
            dma((pairs,)), dma((pairs,)),
            dma((pairs,)), dma((pairs,)),
            dma((blocks,)), dma((blocks,)),
        ],
        compiler_params=pltpu.CompilerParams(
            collective_id=0, has_side_effects=True, vmem_limit_bytes=56 * 1024 * 1024
        ),
    )(
        jnp.broadcast_to(tiles.reshape(-1, 1, 1), (2 * blocks, 1, BLOCK)),
        jnp.broadcast_to(counts.reshape(-1, 1, 1), (blocks, 1, BLOCK)),
        train_emb, val_emb.reshape(val_rows, width),
    )
    return (pot_train.reshape(-1), pot_val.reshape(1, -1), grad_train, grad_val[None])


def solution(mesh):
    return jax.shard_map(
        body,
        mesh=mesh,
        in_specs=(
            P(("groups", "rows"), None),
            P(("groups", "cols"), None, None),
            P(("groups", "rows"), "cols", None),
            P(("groups", "rows")),
        ),
        out_specs=(
            P(("groups", "rows")),
            P(("groups", "cols"), None),
            P(("groups", "rows"), "cols"),
            P(("groups", "cols"), "rows", None),
        ),
        check_vma=False,
    )
```

```python
import functools
import math

import jax
import jax.numpy as jnp
from jax import lax
from jax.experimental import pallas as pl
from jax.experimental.pallas import tpu as pltpu
from jax.sharding import PartitionSpec as P

BLOCK = 512
ITERS = 3
LANES = 128
WEIGHT = 0.1
SCALE = math.log2(math.e) / WEIGHT
FLOOR = -1e30
MESH = pl.DeviceIdType.MESH
STRIPS = BLOCK // LANES
PIECES = 2


def strip(index):
    return pl.ds(index * LANES, LANES)


def diagonal():
    return lax.broadcasted_iota(jnp.int32, (LANES, LANES), 0) == lax.broadcasted_iota(
        jnp.int32, (LANES, LANES), 1
    )


def to_row(column):
    return jnp.sum(
        jnp.where(diagonal(), jnp.broadcast_to(column, (LANES, LANES)), 0.0), axis=0, keepdims=True
    )


def to_column(row):
    return jnp.sum(
        jnp.where(diagonal(), jnp.broadcast_to(row, (LANES, LANES)), 0.0), axis=1, keepdims=True
    )


def kernel(
    n, blocks, vals,
    tiles_ref, counts_ref, x_ref, y_ref,
    pot_train_ref, pot_val_ref, grad_train_ref, grad_val_ref,
    cost, plan, chosen, val_sq, g_ref, f_wide, mass_wide, tile_top, tile_sum, row_part,
    row_box, val_box, parts_sum, paired, landed, term_out, term_in,
    mate_in, core_in, mate_x, mate_tiles, mate_f, f_keep,
    row_send, row_recv, val_send, val_recv, pair_send, pair_recv, own_send, own_recv,
    term_send, term_recv, mate_send, mate_recv, core_send, core_recv, small_send, small_recv,
):
    me = lax.axis_index("rows")
    core = lax.axis_index("cols")
    other = 1 - core
    width = x_ref.shape[1]
    half_width = width // 2
    live_total = blocks * n * (3 * BLOCK // 4)
    val_total = vals * BLOCK * 2
    quads = n // 4
    share = vals * BLOCK // n
    piece = share // PIECES
    span_width = 2 * share
    quad = lax.div(me, 4)
    part = lax.rem(lax.div(me, 2), 2)
    side = lax.rem(me, 2)
    mate = quad * 4 + (1 - part) * 2 + side
    twin = quad * 4 + part * 2 + 1 - side

    barrier = pltpu.get_barrier_semaphore()

    @pl.loop(1, n)
    def _(d):
        pl.semaphore_signal(
            barrier, inc=1, device_id={"rows": lax.rem(me + d, n)}, device_id_type=MESH
        )

    pl.semaphore_signal(barrier, inc=1, device_id={"cols": other}, device_id_type=MESH)
    pl.semaphore_wait(barrier, n)

    def pick(q, rows_of, spare):
        found = rows_of(0)
        for v in range(1, vals):
            found = jnp.where(tiles_ref[q][:, 0:spare] == v, rows_of(v), found)
        return found

    def g_of(q):
        return pick(q, lambda v: g_ref[v], BLOCK)

    def block_rows(index):
        return pl.ds(pl.multiple_of(index * BLOCK, BLOCK), BLOCK)

    def mate_copy(t):
        return pltpu.make_async_remote_copy(
            src_ref=term_out.at[t], dst_ref=mate_in.at[t],
            send_sem=mate_send.at[t], recv_sem=mate_recv.at[t],
            device_id={"rows": mate}, device_id_type=MESH,
        )

    def core_copy(t):
        return pltpu.make_async_remote_copy(
            src_ref=mate_in.at[t], dst_ref=core_in.at[t],
            send_sem=core_send.at[t], recv_sem=core_recv.at[t],
            device_id={"cols": other}, device_id_type=MESH,
        )

    def small_copy(index, source, target):
        return pltpu.make_async_remote_copy(
            src_ref=source, dst_ref=target,
            send_sem=small_send.at[index], recv_sem=small_recv.at[index],
            device_id={"rows": mate}, device_id_type=MESH,
        )

    def half_of(which):
        return pl.ds(pl.multiple_of(which * half_width, LANES), half_width)

    tile_copy = small_copy(0, tiles_ref, mate_tiles)
    tile_copy.start()

    @pl.loop(0, blocks)
    def _(t):
        term_out[t] = x_ref[block_rows(t), half_of(core)].astype(jnp.float32)
        mate_copy(t).start()

    for v in range(vals):
        for c in range(STRIPS):
            rows = y_ref[pl.ds(v * BLOCK + c * LANES, LANES), :].astype(jnp.float32)
            val_sq[v, :, strip(c)] = to_row(jnp.sum(rows * rows, axis=1, keepdims=True))

    @pl.loop(0, blocks)
    def _(t):
        x = x_ref[block_rows(t), :]
        xf = x.astype(jnp.float32)
        x_sq = jnp.sum(xf * xf, axis=1, keepdims=True)
        for k in range(2):
            q = t * 2 + k
            for j in range(width // LANES):
                chosen[q, :, strip(j)] = pick(
                    q, lambda v: y_ref[v * BLOCK : (v + 1) * BLOCK, strip(j)], LANES
                )
            inner = lax.dot_general(
                x, chosen[q], (((1,), (1,)), ((), ())),
                preferred_element_type=jnp.float32,
            )
            cost[t * 2 + k] = ((x_sq + pick(q, lambda v: val_sq[v], BLOCK)) - 2.0 * inner) * SCALE

    g_ref[...] = jnp.zeros_like(g_ref)

    def val_copy(it, peer, slot):
        return pltpu.make_async_remote_copy(
            src_ref=val_box.at[it, slot], dst_ref=val_box.at[it, slot],
            send_sem=val_send.at[it, peer], recv_sem=val_recv.at[it, slot],
            device_id={"rows": peer}, device_id_type=MESH,
        )

    @pl.loop(0, ITERS)
    def _(it):
        @pl.loop(0, blocks)
        def _(t):
            g = [g_of(t * 2 + k) for k in range(2)]
            for c in range(STRIPS):
                def score(k, j):
                    return g[k][:, j * LANES : (j + 1) * LANES] - cost[t * 2 + k, strip(c), strip(j)]
                top = jnp.full((LANES, LANES), FLOOR, jnp.float32)
                for k in range(2):
                    for j in range(STRIPS):
                        top = jnp.maximum(top, score(k, j))
                top = jnp.max(top, axis=1, keepdims=True)
                wide = jnp.broadcast_to(top, (LANES, LANES))
                total = jnp.zeros((LANES, LANES), jnp.float32)
                for k in range(2):
                    for j in range(STRIPS):
                        total = total + jnp.exp2(score(k, j) - wide)
                total = jnp.sum(total, axis=1, keepdims=True)
                row_part[t, :, strip(c)] = to_row(top)
                row_part[blocks + t, :, strip(c)] = to_row(total)

        for q in range(2 * blocks):
            row_box[it, core, q : q + 1, :] = row_part[q]
        out = pltpu.make_async_remote_copy(
            src_ref=row_box.at[it, core], dst_ref=row_box.at[it, core],
            send_sem=row_send.at[it], recv_sem=row_recv.at[it],
            device_id={"cols": other}, device_id_type=MESH,
        )
        out.start()
        out.wait()
        tops = [row_box[it, q, 0:blocks, :] for q in range(2)]
        top = jnp.maximum(tops[0], tops[1])
        total = sum(
            row_box[it, q, blocks : 2 * blocks, :] * jnp.exp2(tops[q] - top) for q in range(2)
        )
        f_all = math.log2(1.0 / live_total) - (top + jnp.log2(total))
        lane = lax.broadcasted_iota(jnp.int32, (1, BLOCK), 1)
        for t in range(blocks):
            live = lane < counts_ref[t]
            pot_train_ref[t : t + 1, :] = jnp.where(live, f_all[t : t + 1] * (1.0 / SCALE), 0.0)
            f = jnp.where(live, f_all[t : t + 1], FLOOR)
            f_keep[t : t + 1, :] = f
            for c in range(STRIPS):
                f_wide[pl.ds(t * BLOCK + c * LANES, LANES), :] = jnp.broadcast_to(
                    to_column(f[:, c * LANES : (c + 1) * LANES]), (LANES, LANES)
                )

        @pl.loop(0, blocks)
        def _(t):
            for k in range(2):
                for c in range(STRIPS):
                    score = f_wide[block_rows(t), :] - cost[t * 2 + k, :, strip(c)]
                    top = jnp.max(score, axis=0, keepdims=True)
                    total = jnp.sum(jnp.exp2(score - top), axis=0, keepdims=True)
                    tile_top[t * 2 + k, :, strip(c)] = top
                    tile_sum[t * 2 + k, :, strip(c)] = total

        for v in range(vals):
            top = jnp.full((1, BLOCK), FLOOR, jnp.float32)
            for q in range(2 * blocks):
                top = jnp.maximum(top, jnp.where(tiles_ref[q] == v, tile_top[q], FLOOR))
            total = jnp.zeros((1, BLOCK), jnp.float32)
            for q in range(2 * blocks):
                scaled = tile_sum[q] * jnp.exp2(jnp.minimum(tile_top[q] - top, 0.0))
                total = total + jnp.where(tiles_ref[q] == v, scaled, 0.0)
            val_box[it, me, v : v + 1, :] = top
            val_box[it, me, vals + v : vals + v + 1, :] = total

        @pl.loop(1, n)
        def _(d):
            val_copy(it, lax.rem(me + d, n), me).start()

        @pl.loop(1, n)
        def _(d):
            val_copy(it, lax.rem(me + d, n), lax.rem(me + d, n)).wait_recv()

        top = val_box[it, 0, 0:vals, :]
        for q in range(1, n):
            top = jnp.maximum(top, val_box[it, q, 0:vals, :])
        total = jnp.zeros((vals, BLOCK), jnp.float32)
        for q in range(n):
            total = total + val_box[it, q, vals : 2 * vals, :] * jnp.exp2(val_box[it, q, 0:vals, :] - top)
        g = math.log2(1.0 / val_total) - (top + jnp.log2(total))
        pot_val_ref[...] = g * (1.0 / SCALE)
        for v in range(vals):
            g_ref[v] = g[v : v + 1]
        mate_copy(it).wait_recv()
        core_copy(it).start()

    f_copy = small_copy(1, f_keep, mate_f)
    f_copy.start()

    @pl.loop(0, blocks)
    def _(t):
        g = [g_of(t * 2 + k) for k in range(2)]
        for c in range(STRIPS):
            f = f_wide[pl.ds(pl.multiple_of(t * BLOCK + c * LANES, LANES), LANES), :]
            total = jnp.zeros((LANES, LANES), jnp.float32)
            for k in range(2):
                for j in range(STRIPS):
                    value = jnp.exp2(
                        f + g[k][:, j * LANES : (j + 1) * LANES] - cost[t * 2 + k, strip(c), strip(j)]
                    )
                    total = total + value
                    plan[t * 2 + k, strip(c), strip(j)] = value.astype(jnp.bfloat16)
            mass_wide[pl.ds(pl.multiple_of(t * BLOCK + c * LANES, LANES), LANES), :] = (
                jnp.broadcast_to(jnp.sum(total, axis=1, keepdims=True), (LANES, LANES))
            )

    def rows_of_piece(j):
        return pl.ds(pl.multiple_of(j * piece, piece), piece)

    def pair_copy(s, j):
        return pltpu.make_async_remote_copy(
            src_ref=parts_sum.at[s, 1 - side, rows_of_piece(j)],
            dst_ref=paired.at[s, rows_of_piece(j)],
            send_sem=pair_send.at[s, j], recv_sem=pair_recv.at[s, j],
            device_id={"rows": twin}, device_id_type=MESH,
        )

    def own_copy(s, slot, j):
        goal = lax.rem(quad + 1 + s, quads)
        return pltpu.make_async_remote_copy(
            src_ref=parts_sum.at[s, side, rows_of_piece(j)],
            dst_ref=landed.at[slot, rows_of_piece(j)],
            send_sem=own_send.at[s, j], recv_sem=own_recv.at[slot, j],
            device_id={"rows": goal * 4 + part * 2 + side}, device_id_type=MESH,
        )

    def term_copy(t):
        return pltpu.make_async_remote_copy(
            src_ref=term_out.at[t], dst_ref=term_in.at[t],
            send_sem=term_send.at[t], recv_sem=term_recv.at[t],
            device_id={"cols": other}, device_id_type=MESH,
        )

    @pl.loop(0, blocks)
    def _(t):
        mass = mass_wide[block_rows(t), 0:1]

        def pull(which):
            span = half_of(which)
            total = mass * x_ref[block_rows(t), span].astype(jnp.float32)
            pulled = sum(
                jnp.dot(
                    plan[t * 2 + k], chosen[t * 2 + k, :, span],
                    preferred_element_type=jnp.float32,
                )
                for k in range(2)
            )
            return total - pulled

        mate_copy(t).wait_send()
        term_out[t] = pull(other)
        term_copy(t).start()
        cost[t, :, 0:half_width] = pull(core)

    tile_copy.wait()
    f_copy.wait()
    for t in range(blocks):
        for c in range(STRIPS):
            f_wide[pl.ds(t * BLOCK + c * LANES, LANES), :] = jnp.broadcast_to(
                to_column(mate_f[t : t + 1, strip(c)]), (LANES, LANES)
            )

    @pl.loop(ITERS, blocks)
    def _(t):
        mate_copy(t).wait_recv()
        core_copy(t).start()

    @pl.loop(0, blocks)
    def _(t):
        core_copy(t).wait()
        mate_x[block_rows(t), half_of(core)] = mate_in[t].astype(jnp.bfloat16)
        mate_x[block_rows(t), half_of(other)] = core_in[t].astype(jnp.bfloat16)

    @pl.loop(0, quads)
    def _(s):
        goal = lax.rem(quad + 1 + s, quads)
        start = (goal * 4 + part * 2) * share
        v = lax.div(start, BLOCK)
        span = pl.ds(pl.multiple_of(lax.rem(start, BLOCK), span_width), span_width)
        y = y_ref[pl.ds(pl.multiple_of(start, span_width), span_width), :]
        y_sq = val_sq[v, :, span]
        g = g_ref[v, :, span]
        parts_sum[s] = jnp.zeros((2, share, width), jnp.float32)

        @pl.loop(0, blocks)
        def _(t):
            first = plan[t * 2, :, span]
            second = plan[t * 2 + 1, :, span]
            own = jnp.where(
                tiles_ref[t * 2][:, 0:span_width] == v, first,
                jnp.where(tiles_ref[t * 2 + 1][:, 0:span_width] == v, second, jnp.zeros_like(first)),
            )
            total = lax.dot_general(
                own, x_ref[block_rows(t), :], (((0,), (0,)), ((), ())),
                preferred_element_type=jnp.float32,
            )
            x = mate_x[block_rows(t), :]
            xf = x.astype(jnp.float32)
            x_sq = jnp.sum(xf * xf, axis=1, keepdims=True)
            inner = lax.dot_general(
                x, y, (((1,), (1,)), ((), ())), preferred_element_type=jnp.float32
            )
            met = jnp.logical_or(
                mate_tiles[t * 2][:, 0:span_width] == v, mate_tiles[t * 2 + 1][:, 0:span_width] == v
            )
            value = jnp.exp2(
                f_wide[block_rows(t), 0:1] + jnp.where(met, g, FLOOR)
                - ((x_sq + y_sq) - 2.0 * inner) * SCALE
            )
            total = total + lax.dot_general(
                value.astype(jnp.bfloat16), x, (((0,), (0,)), ((), ())),
                preferred_element_type=jnp.float32,
            )
            parts_sum[s, 0] = parts_sum[s, 0] + total[0:share]
            parts_sum[s, 1] = parts_sum[s, 1] + total[share:]

        @pl.loop(0, PIECES)
        def _(j):
            pair_copy(s, j).start()

    @pl.loop(0, quads - 1)
    def _(s):
        @pl.loop(0, PIECES)
        def _(j):
            pair_copy(s, j).wait_recv()
            at = rows_of_piece(j)
            parts_sum[s, side, at] = parts_sum[s, side, at] + paired[s, at]
            own_copy(s, quad, j).start()

    @pl.loop(0, blocks)
    def _(t):
        term_copy(t).wait()
        grad_train_ref[block_rows(t), :] = (
            live_total * 2.0 * (cost[t, :, 0:half_width] + term_in[t])
        ).astype(jnp.bfloat16)

    @pl.loop(0, PIECES)
    def _(j):
        pair_copy(quads - 1, j).wait_recv()

    own_rows = y_ref[pl.ds(pl.multiple_of(me * share, share), share), :].astype(jnp.float32)
    grad_val_ref[...] = parts_sum[quads - 1, side] + paired[quads - 1]

    @pl.loop(0, quads - 1)
    def _(s):
        slot = lax.rem(quad + 1 + s, quads)

        @pl.loop(0, PIECES)
        def _(j):
            own_copy(s, slot, j).wait_recv()

        grad_val_ref[...] = grad_val_ref[...] + landed[slot]

    grad_val_ref[...] = 2.0 * (own_rows - val_total * grad_val_ref[...])

    @pl.loop(0, PIECES)
    def _(j):
        @pl.loop(0, quads)
        def _(s):
            pair_copy(s, j).wait_send()

        @pl.loop(0, quads - 1)
        def _(s):
            own_copy(s, quad, j).wait_send()

    @pl.loop(0, ITERS)
    def _(it):
        @pl.loop(1, n)
        def _(d):
            val_copy(it, lax.rem(me + d, n), me).wait_send()


def body(train_emb, val_emb, tiles, counts):
    n = lax.axis_size("rows")
    rows, width = train_emb.shape
    blocks = counts.shape[0]
    val_rows = val_emb.shape[1]
    vals = val_rows // BLOCK
    share = val_rows // n
    quads = n // 4
    half = width // 2
    f32, bf16 = jnp.float32, jnp.bfloat16
    dma = pltpu.SemaphoreType.DMA
    vmem = pl.BlockSpec(memory_space=pltpu.VMEM)
    pot_train, pot_val, grad_train, grad_val = pl.pallas_call(
        functools.partial(kernel, n, blocks, vals),
        out_shape=(
            jax.ShapeDtypeStruct((blocks, BLOCK), f32),
            jax.ShapeDtypeStruct((vals, BLOCK), f32),
            jax.ShapeDtypeStruct((rows, half), bf16),
            jax.ShapeDtypeStruct((share, width), f32),
        ),
        in_specs=[vmem, vmem, vmem, vmem],
        out_specs=(vmem, vmem, vmem, vmem),
        scratch_shapes=[
            pltpu.VMEM((2 * blocks, BLOCK, BLOCK), f32),
            pltpu.VMEM((2 * blocks, BLOCK, BLOCK), bf16),
            pltpu.VMEM((2 * blocks, BLOCK, width), bf16),
            pltpu.VMEM((vals, 1, BLOCK), f32),
            pltpu.VMEM((vals, 1, BLOCK), f32),
            pltpu.VMEM((rows, LANES), f32),
            pltpu.VMEM((rows, LANES), f32),
            pltpu.VMEM((2 * blocks, 1, BLOCK), f32),
            pltpu.VMEM((2 * blocks, 1, BLOCK), f32),
            pltpu.VMEM((2 * blocks, 1, BLOCK), f32),
            pltpu.VMEM((ITERS, 2, 2 * blocks, BLOCK), f32),
            pltpu.VMEM((ITERS, n, 2 * vals, BLOCK), f32),
            pltpu.VMEM((quads, 2, share, width), f32),
            pltpu.VMEM((quads, share, width), f32),
            pltpu.VMEM((quads, share, width), f32),
            pltpu.VMEM((blocks, BLOCK, half), f32),
            pltpu.VMEM((blocks, BLOCK, half), f32),
            pltpu.VMEM((blocks, BLOCK, half), f32),
            pltpu.VMEM((blocks, BLOCK, half), f32),
            pltpu.VMEM((rows, width), bf16),
            pltpu.VMEM((2 * blocks, 1, BLOCK), jnp.int32),
            pltpu.VMEM((blocks, BLOCK), f32),
            pltpu.VMEM((blocks, BLOCK), f32),
            dma((ITERS,)), dma((ITERS,)),
            dma((ITERS, n)), dma((ITERS, n)),
            dma((quads, PIECES)), dma((quads, PIECES)),
            dma((quads, PIECES)), dma((quads, PIECES)),
            dma((blocks,)), dma((blocks,)),
            dma((blocks,)), dma((blocks,)),
            dma((blocks,)), dma((blocks,)),
            dma((2,)), dma((2,)),
        ],
        compiler_params=pltpu.CompilerParams(
            collective_id=0, has_side_effects=True, vmem_limit_bytes=60 * 1024 * 1024
        ),
    )(
        jnp.broadcast_to(tiles.reshape(-1, 1, 1), (2 * blocks, 1, BLOCK)),
        jnp.broadcast_to(counts.reshape(-1, 1, 1), (blocks, 1, BLOCK)),
        train_emb, val_emb.reshape(val_rows, width),
    )
    return (pot_train.reshape(-1), pot_val.reshape(1, -1), grad_train, grad_val[None])


def solution(mesh):
    return jax.shard_map(
        body,
        mesh=mesh,
        in_specs=(
            P(("groups", "rows"), None),
            P(("groups", "cols"), None, None),
            P(("groups", "rows"), "cols", None),
            P(("groups", "rows")),
        ),
        out_specs=(
            P(("groups", "rows")),
            P(("groups", "cols"), None),
            P(("groups", "rows"), "cols"),
            P(("groups", "cols"), "rows", None),
        ),
        check_vma=False,
    )
```

```python
import functools
import math

import jax
import jax.numpy as jnp
from jax import lax
from jax.experimental import pallas as pl
from jax.experimental.pallas import tpu as pltpu
from jax.sharding import PartitionSpec as P

BLOCK = 512
ITERS = 3
LANES = 128
WEIGHT = 0.1
SCALE = math.log2(math.e) / WEIGHT
FLOOR = -1e30
MESH = pl.DeviceIdType.MESH
STRIPS = BLOCK // LANES
PIECES = 4


def strip(index):
    return pl.ds(index * LANES, LANES)


def diagonal():
    return lax.broadcasted_iota(jnp.int32, (LANES, LANES), 0) == lax.broadcasted_iota(
        jnp.int32, (LANES, LANES), 1
    )


def to_row(column):
    return jnp.sum(
        jnp.where(diagonal(), jnp.broadcast_to(column, (LANES, LANES)), 0.0), axis=0, keepdims=True
    )


def to_column(row):
    return jnp.sum(
        jnp.where(diagonal(), jnp.broadcast_to(row, (LANES, LANES)), 0.0), axis=1, keepdims=True
    )


def kernel(
    n, blocks, vals,
    tiles_ref, counts_ref, x_ref, y_ref,
    pot_train_ref, pot_val_ref, grad_train_ref, grad_val_ref,
    cost, plan, chosen, val_sq, g_ref, f_wide, mass_wide, tile_top, tile_sum, row_part,
    row_box, val_box, away, home, paired, landed, term_out, term_in,
    row_send, row_recv, val_send, val_recv, pair_send, pair_recv, own_send, own_recv,
    term_send, term_recv,
):
    me = lax.axis_index("rows")
    core = lax.axis_index("cols")
    other = 1 - core
    width = x_ref.shape[1]
    half_width = width // 2
    live_total = blocks * n * (3 * BLOCK // 4)
    val_total = vals * BLOCK * 2
    pairs = n // 2
    share = vals * BLOCK // n
    stage = lax.div(me, 2)
    side = lax.rem(me, 2)
    mate = stage * 2 + 1 - side

    barrier = pltpu.get_barrier_semaphore()

    @pl.loop(1, n)
    def _(d):
        pl.semaphore_signal(
            barrier, inc=1, device_id={"rows": lax.rem(me + d, n)}, device_id_type=MESH
        )

    pl.semaphore_signal(barrier, inc=1, device_id={"cols": other}, device_id_type=MESH)
    pl.semaphore_wait(barrier, n)

    def pick(q, rows_of, spare):
        found = rows_of(0)
        for v in range(1, vals):
            found = jnp.where(tiles_ref[q][:, 0:spare] == v, rows_of(v), found)
        return found

    def g_of(q):
        return pick(q, lambda v: g_ref[v], BLOCK)

    def block_rows(index):
        return pl.ds(pl.multiple_of(index * BLOCK, BLOCK), BLOCK)

    for v in range(vals):
        for c in range(STRIPS):
            rows = y_ref[pl.ds(v * BLOCK + c * LANES, LANES), :].astype(jnp.float32)
            val_sq[v, :, strip(c)] = to_row(jnp.sum(rows * rows, axis=1, keepdims=True))

    @pl.loop(0, blocks)
    def _(t):
        x = x_ref[block_rows(t), :]
        xf = x.astype(jnp.float32)
        x_sq = jnp.sum(xf * xf, axis=1, keepdims=True)
        for k in range(2):
            q = t * 2 + k
            for j in range(width // LANES):
                chosen[q, :, strip(j)] = pick(
                    q, lambda v: y_ref[v * BLOCK : (v + 1) * BLOCK, strip(j)], LANES
                )
            inner = lax.dot_general(
                x, chosen[q], (((1,), (1,)), ((), ())),
                preferred_element_type=jnp.float32,
            )
            cost[t * 2 + k] = ((x_sq + pick(q, lambda v: val_sq[v], BLOCK)) - 2.0 * inner) * SCALE

    g_ref[...] = jnp.zeros_like(g_ref)

    def val_copy(it, peer, slot):
        return pltpu.make_async_remote_copy(
            src_ref=val_box.at[it, slot], dst_ref=val_box.at[it, slot],
            send_sem=val_send.at[it, peer], recv_sem=val_recv.at[it, slot],
            device_id={"rows": peer}, device_id_type=MESH,
        )

    @pl.loop(0, ITERS)
    def _(it):
        @pl.loop(0, blocks)
        def _(t):
            g = [g_of(t * 2 + k) for k in range(2)]
            for c in range(STRIPS):
                def score(k, j):
                    return g[k][:, j * LANES : (j + 1) * LANES] - cost[t * 2 + k, strip(c), strip(j)]
                top = jnp.full((LANES, LANES), FLOOR, jnp.float32)
                for k in range(2):
                    for j in range(STRIPS):
                        top = jnp.maximum(top, score(k, j))
                top = jnp.max(top, axis=1, keepdims=True)
                wide = jnp.broadcast_to(top, (LANES, LANES))
                total = jnp.zeros((LANES, LANES), jnp.float32)
                for k in range(2):
                    for j in range(STRIPS):
                        total = total + jnp.exp2(score(k, j) - wide)
                total = jnp.sum(total, axis=1, keepdims=True)
                row_part[t, :, strip(c)] = to_row(top)
                row_part[blocks + t, :, strip(c)] = to_row(total)

        for q in range(2 * blocks):
            row_box[it, core, q : q + 1, :] = row_part[q]
        out = pltpu.make_async_remote_copy(
            src_ref=row_box.at[it, core], dst_ref=row_box.at[it, core],
            send_sem=row_send.at[it], recv_sem=row_recv.at[it],
            device_id={"cols": other}, device_id_type=MESH,
        )
        out.start()
        out.wait()
        tops = [row_box[it, q, 0:blocks, :] for q in range(2)]
        top = jnp.maximum(tops[0], tops[1])
        total = sum(
            row_box[it, q, blocks : 2 * blocks, :] * jnp.exp2(tops[q] - top) for q in range(2)
        )
        f_all = math.log2(1.0 / live_total) - (top + jnp.log2(total))
        lane = lax.broadcasted_iota(jnp.int32, (1, BLOCK), 1)
        for t in range(blocks):
            live = lane < counts_ref[t]
            pot_train_ref[t : t + 1, :] = jnp.where(live, f_all[t : t + 1] * (1.0 / SCALE), 0.0)
            f = jnp.where(live, f_all[t : t + 1], FLOOR)
            for c in range(STRIPS):
                f_wide[pl.ds(t * BLOCK + c * LANES, LANES), :] = jnp.broadcast_to(
                    to_column(f[:, c * LANES : (c + 1) * LANES]), (LANES, LANES)
                )

        @pl.loop(0, blocks)
        def _(t):
            for k in range(2):
                for c in range(STRIPS):
                    score = f_wide[block_rows(t), :] - cost[t * 2 + k, :, strip(c)]
                    top = jnp.max(score, axis=0, keepdims=True)
                    total = jnp.sum(jnp.exp2(score - top), axis=0, keepdims=True)
                    tile_top[t * 2 + k, :, strip(c)] = top
                    tile_sum[t * 2 + k, :, strip(c)] = total

        for v in range(vals):
            top = jnp.full((1, BLOCK), FLOOR, jnp.float32)
            for q in range(2 * blocks):
                top = jnp.maximum(top, jnp.where(tiles_ref[q] == v, tile_top[q], FLOOR))
            total = jnp.zeros((1, BLOCK), jnp.float32)
            for q in range(2 * blocks):
                scaled = tile_sum[q] * jnp.exp2(jnp.minimum(tile_top[q] - top, 0.0))
                total = total + jnp.where(tiles_ref[q] == v, scaled, 0.0)
            val_box[it, me, v : v + 1, :] = top
            val_box[it, me, vals + v : vals + v + 1, :] = total

        @pl.loop(1, n)
        def _(d):
            val_copy(it, lax.rem(me + d, n), me).start()

        @pl.loop(1, n)
        def _(d):
            val_copy(it, lax.rem(me + d, n), lax.rem(me + d, n)).wait_recv()

        top = val_box[it, 0, 0:vals, :]
        for q in range(1, n):
            top = jnp.maximum(top, val_box[it, q, 0:vals, :])
        total = jnp.zeros((vals, BLOCK), jnp.float32)
        for q in range(n):
            total = total + val_box[it, q, vals : 2 * vals, :] * jnp.exp2(val_box[it, q, 0:vals, :] - top)
        g = math.log2(1.0 / val_total) - (top + jnp.log2(total))
        pot_val_ref[...] = g * (1.0 / SCALE)
        for v in range(vals):
            g_ref[v] = g[v : v + 1]

    @pl.loop(0, blocks)
    def _(t):
        g = [g_of(t * 2 + k) for k in range(2)]
        for c in range(STRIPS):
            f = f_wide[pl.ds(pl.multiple_of(t * BLOCK + c * LANES, LANES), LANES), :]
            total = jnp.zeros((LANES, LANES), jnp.float32)
            for k in range(2):
                for j in range(STRIPS):
                    value = jnp.exp2(
                        f + g[k][:, j * LANES : (j + 1) * LANES] - cost[t * 2 + k, strip(c), strip(j)]
                    )
                    total = total + value
                    plan[t * 2 + k, strip(c), strip(j)] = value.astype(jnp.bfloat16)
            mass_wide[pl.ds(pl.multiple_of(t * BLOCK + c * LANES, LANES), LANES), :] = (
                jnp.broadcast_to(jnp.sum(total, axis=1, keepdims=True), (LANES, LANES))
            )

    piece = share // PIECES

    def rows_of(j):
        return pl.ds(pl.multiple_of(j * piece, piece), piece)

    def pair_copy(s, j):
        return pltpu.make_async_remote_copy(
            src_ref=away.at[s, rows_of(j)], dst_ref=paired.at[s, rows_of(j)],
            send_sem=pair_send.at[s, j], recv_sem=pair_recv.at[s, j],
            device_id={"rows": mate}, device_id_type=MESH,
        )

    def own_copy(s, slot, j):
        goal = lax.rem(stage + 1 + s, pairs)
        return pltpu.make_async_remote_copy(
            src_ref=home.at[s, rows_of(j)], dst_ref=landed.at[slot, rows_of(j)],
            send_sem=own_send.at[s, j], recv_sem=own_recv.at[slot, j],
            device_id={"rows": goal * 2 + side}, device_id_type=MESH,
        )

    def merge_piece(s, j):
        pair_copy(s, j).wait_recv()
        home[s, rows_of(j)] = home[s, rows_of(j)] + paired[s, rows_of(j)]

    def relay(s):
        @pl.loop(0, PIECES)
        def _(j):
            merge_piece(s, j)
            own_copy(s, stage, j).start()

    def term_copy(t):
        return pltpu.make_async_remote_copy(
            src_ref=term_out.at[t], dst_ref=term_in.at[t],
            send_sem=term_send.at[t], recv_sem=term_recv.at[t],
            device_id={"cols": other}, device_id_type=MESH,
        )

    @pl.loop(0, pairs)
    def _(s):
        goal = lax.rem(stage + 1 + s, pairs)

        def push(which):
            start = (goal * 2 + which) * share
            v = lax.div(start, BLOCK)
            inside = lax.rem(start, BLOCK)
            total = jnp.zeros((share, width), jnp.float32)
            for t in range(blocks):
                if share % LANES == 0:
                    span = pl.ds(pl.multiple_of(inside, share), share)
                    parts = [plan[t * 2 + k, :, span] for k in range(2)]
                    offset = None
                else:
                    base = lax.div(inside, LANES) * LANES
                    span = pl.ds(pl.multiple_of(base, LANES), LANES)
                    parts = [plan[t * 2 + k, :, span] for k in range(2)]
                    offset = inside - base
                zero = jnp.zeros_like(parts[0])
                picked = jnp.where(
                    tiles_ref[t * 2][:, 0 : zero.shape[1]] == v, parts[0],
                    jnp.where(tiles_ref[t * 2 + 1][:, 0 : zero.shape[1]] == v, parts[1], zero),
                )
                product = lax.dot_general(
                    picked, x_ref[t * BLOCK : (t + 1) * BLOCK, :], (((0,), (0,)), ((), ())),
                    preferred_element_type=jnp.float32,
                )
                if offset is not None:
                    keep = product[0:share]
                    for piece in range(1, LANES // share):
                        keep = jnp.where(
                            offset == piece * share, product[piece * share : (piece + 1) * share], keep
                        )
                    product = keep
                total = total + product
            return total

        away[s] = push(1 - side)

        @pl.loop(0, PIECES)
        def _(j):
            pair_copy(s, j).start()

        home[s] = push(side)

    relay(0)

    @pl.loop(0, blocks)
    def _(t):
        mass = mass_wide[block_rows(t), 0:1]

        def pull(which):
            span = pl.ds(pl.multiple_of(which * half_width, LANES), half_width)
            total = mass * x_ref[block_rows(t), span].astype(jnp.float32)
            pulled = sum(
                jnp.dot(
                    plan[t * 2 + k], chosen[t * 2 + k, :, span],
                    preferred_element_type=jnp.float32,
                )
                for k in range(2)
            )
            return total - pulled

        term_out[t] = pull(other)
        term_copy(t).start()
        cost[t, :, 0:half_width] = pull(core)

    @pl.loop(1, pairs - 1)
    def _(s):
        relay(s)

    @pl.loop(0, blocks)
    def _(t):
        term_copy(t).wait()
        grad_train_ref[block_rows(t), :] = (
            live_total * 2.0 * (cost[t, :, 0:half_width] + term_in[t])
        ).astype(jnp.bfloat16)

    @pl.loop(0, PIECES)
    def _(j):
        merge_piece(pairs - 1, j)

    @pl.loop(0, pairs - 1)
    def _(s):
        slot = lax.rem(stage + 1 + s, pairs)

        @pl.loop(0, PIECES)
        def _(j):
            own_copy(s, slot, j).wait_recv()

        home[pairs - 1] = home[pairs - 1] + landed[slot]

    own_rows = y_ref[pl.ds(pl.multiple_of(me * share, share), share), :].astype(jnp.float32)
    grad_val_ref[...] = 2.0 * (own_rows - val_total * home[pairs - 1])

    @pl.loop(0, PIECES)
    def _(j):
        @pl.loop(0, pairs)
        def _(s):
            pair_copy(s, j).wait_send()

        @pl.loop(0, pairs - 1)
        def _(s):
            own_copy(s, stage, j).wait_send()

    @pl.loop(0, ITERS)
    def _(it):
        @pl.loop(1, n)
        def _(d):
            val_copy(it, lax.rem(me + d, n), me).wait_send()


def body(train_emb, val_emb, tiles, counts):
    n = lax.axis_size("rows")
    rows, width = train_emb.shape
    blocks = counts.shape[0]
    val_rows = val_emb.shape[1]
    vals = val_rows // BLOCK
    share = val_rows // n
    pairs = n // 2
    half = width // 2
    f32, bf16 = jnp.float32, jnp.bfloat16
    dma = pltpu.SemaphoreType.DMA
    vmem = pl.BlockSpec(memory_space=pltpu.VMEM)
    pot_train, pot_val, grad_train, grad_val = pl.pallas_call(
        functools.partial(kernel, n, blocks, vals),
        out_shape=(
            jax.ShapeDtypeStruct((blocks, BLOCK), f32),
            jax.ShapeDtypeStruct((vals, BLOCK), f32),
            jax.ShapeDtypeStruct((rows, half), bf16),
            jax.ShapeDtypeStruct((share, width), f32),
        ),
        in_specs=[vmem, vmem, vmem, vmem],
        out_specs=(vmem, vmem, vmem, vmem),
        scratch_shapes=[
            pltpu.VMEM((2 * blocks, BLOCK, BLOCK), f32),
            pltpu.VMEM((2 * blocks, BLOCK, BLOCK), bf16),
            pltpu.VMEM((2 * blocks, BLOCK, width), bf16),
            pltpu.VMEM((vals, 1, BLOCK), f32),
            pltpu.VMEM((vals, 1, BLOCK), f32),
            pltpu.VMEM((rows, LANES), f32),
            pltpu.VMEM((rows, LANES), f32),
            pltpu.VMEM((2 * blocks, 1, BLOCK), f32),
            pltpu.VMEM((2 * blocks, 1, BLOCK), f32),
            pltpu.VMEM((2 * blocks, 1, BLOCK), f32),
            pltpu.VMEM((ITERS, 2, 2 * blocks, BLOCK), f32),
            pltpu.VMEM((ITERS, n, 2 * vals, BLOCK), f32),
            pltpu.VMEM((pairs, share, width), f32),
            pltpu.VMEM((pairs, share, width), f32),
            pltpu.VMEM((pairs, share, width), f32),
            pltpu.VMEM((pairs, share, width), f32),
            pltpu.VMEM((blocks, BLOCK, half), f32),
            pltpu.VMEM((blocks, BLOCK, half), f32),
            dma((ITERS,)), dma((ITERS,)),
            dma((ITERS, n)), dma((ITERS, n)),
            dma((pairs, PIECES)), dma((pairs, PIECES)),
            dma((pairs, PIECES)), dma((pairs, PIECES)),
            dma((blocks,)), dma((blocks,)),
        ],
        compiler_params=pltpu.CompilerParams(
            collective_id=0, has_side_effects=True, vmem_limit_bytes=56 * 1024 * 1024
        ),
    )(
        jnp.broadcast_to(tiles.reshape(-1, 1, 1), (2 * blocks, 1, BLOCK)),
        jnp.broadcast_to(counts.reshape(-1, 1, 1), (blocks, 1, BLOCK)),
        train_emb, val_emb.reshape(val_rows, width),
    )
    return (pot_train.reshape(-1), pot_val.reshape(1, -1), grad_train, grad_val[None])


def solution(mesh):
    return jax.shard_map(
        body,
        mesh=mesh,
        in_specs=(
            P(("groups", "rows"), None),
            P(("groups", "cols"), None, None),
            P(("groups", "rows"), "cols", None),
            P(("groups", "rows")),
        ),
        out_specs=(
            P(("groups", "rows")),
            P(("groups", "cols"), None),
            P(("groups", "rows"), "cols"),
            P(("groups", "cols"), "rows", None),
        ),
        check_vma=False,
    )
```

```python
import functools
import math

import jax
import jax.numpy as jnp
from jax import lax
from jax.experimental import pallas as pl
from jax.experimental.pallas import tpu as pltpu
from jax.sharding import PartitionSpec as P

BLOCK = 512
ITERS = 3
LANES = 128
WEIGHT = 0.1
SCALE = math.log2(math.e) / WEIGHT
FLOOR = -1e30
MESH = pl.DeviceIdType.MESH
STRIPS = BLOCK // LANES
PIECES = 8


def strip(index):
    return pl.ds(index * LANES, LANES)


def diagonal():
    return lax.broadcasted_iota(jnp.int32, (LANES, LANES), 0) == lax.broadcasted_iota(
        jnp.int32, (LANES, LANES), 1
    )


def to_row(column):
    return jnp.sum(
        jnp.where(diagonal(), jnp.broadcast_to(column, (LANES, LANES)), 0.0), axis=0, keepdims=True
    )


def to_column(row):
    return jnp.sum(
        jnp.where(diagonal(), jnp.broadcast_to(row, (LANES, LANES)), 0.0), axis=1, keepdims=True
    )


def kernel(
    n, blocks, vals,
    tiles_ref, x_ref, y_ref,
    pot_train_ref, pot_val_ref, grad_train_ref, grad_val_ref,
    cost, plan, chosen, val_sq, g_ref, f_wide, mass_wide, tile_top, tile_sum, row_part,
    row_box, val_box, away, home, paired, landed, term_out, term_in,
    row_send, row_recv, val_send, val_recv, pair_send, pair_recv, own_send, own_recv,
    term_send, term_recv,
):
    me = lax.axis_index("rows")
    core = lax.axis_index("cols")
    other = 1 - core
    width = x_ref.shape[1]
    half_width = width // 2
    live_total = blocks * n * (3 * BLOCK // 4)
    val_total = vals * BLOCK * 2
    pairs = n // 2
    share = vals * BLOCK // n
    stage = lax.div(me, 2)
    side = lax.rem(me, 2)
    mate = stage * 2 + 1 - side

    barrier = pltpu.get_barrier_semaphore()

    @pl.loop(1, n)
    def _(d):
        pl.semaphore_signal(
            barrier, inc=1, device_id={"rows": lax.rem(me + d, n)}, device_id_type=MESH
        )

    pl.semaphore_signal(barrier, inc=1, device_id={"cols": other}, device_id_type=MESH)
    pl.semaphore_wait(barrier, n)

    def pick(q, rows_of, spare):
        found = rows_of(0)
        for v in range(1, vals):
            found = jnp.where(tiles_ref[q][:, 0:spare] == v, rows_of(v), found)
        return found

    def g_of(q):
        return pick(q, lambda v: g_ref[v], BLOCK)

    def block_rows(index):
        return pl.ds(pl.multiple_of(index * BLOCK, BLOCK), BLOCK)

    for v in range(vals):
        for c in range(STRIPS):
            rows = y_ref[pl.ds(v * BLOCK + c * LANES, LANES), :].astype(jnp.float32)
            val_sq[v, :, strip(c)] = to_row(jnp.sum(rows * rows, axis=1, keepdims=True))

    @pl.loop(0, blocks)
    def _(t):
        x = x_ref[block_rows(t), :]
        xf = x.astype(jnp.float32)
        x_sq = jnp.sum(xf * xf, axis=1, keepdims=True)
        for k in range(2):
            q = t * 2 + k
            for j in range(width // LANES):
                chosen[q, :, strip(j)] = pick(
                    q, lambda v: y_ref[v * BLOCK : (v + 1) * BLOCK, strip(j)], LANES
                )
            inner = lax.dot_general(
                x, chosen[q], (((1,), (1,)), ((), ())),
                preferred_element_type=jnp.float32,
            )
            cost[t * 2 + k] = ((x_sq + pick(q, lambda v: val_sq[v], BLOCK)) - 2.0 * inner) * SCALE

    g_ref[...] = jnp.zeros_like(g_ref)

    def val_copy(it, peer, slot):
        return pltpu.make_async_remote_copy(
            src_ref=val_box.at[it, slot], dst_ref=val_box.at[it, slot],
            send_sem=val_send.at[it, peer], recv_sem=val_recv.at[it, slot],
            device_id={"rows": peer}, device_id_type=MESH,
        )

    @pl.loop(0, ITERS)
    def _(it):
        @pl.loop(0, blocks)
        def _(t):
            g = [g_of(t * 2 + k) for k in range(2)]
            for c in range(STRIPS):
                def score(k, j):
                    return g[k][:, j * LANES : (j + 1) * LANES] - cost[t * 2 + k, strip(c), strip(j)]
                top = jnp.full((LANES, LANES), FLOOR, jnp.float32)
                for k in range(2):
                    for j in range(STRIPS):
                        top = jnp.maximum(top, score(k, j))
                top = jnp.max(top, axis=1, keepdims=True)
                wide = jnp.broadcast_to(top, (LANES, LANES))
                total = jnp.zeros((LANES, LANES), jnp.float32)
                for k in range(2):
                    for j in range(STRIPS):
                        total = total + jnp.exp2(score(k, j) - wide)
                total = jnp.sum(total, axis=1, keepdims=True)
                row_part[t, :, strip(c)] = to_row(top)
                row_part[blocks + t, :, strip(c)] = to_row(total)

        for q in range(2 * blocks):
            row_box[it, core, q : q + 1, :] = row_part[q]
        out = pltpu.make_async_remote_copy(
            src_ref=row_box.at[it, core], dst_ref=row_box.at[it, core],
            send_sem=row_send.at[it], recv_sem=row_recv.at[it],
            device_id={"cols": other}, device_id_type=MESH,
        )
        out.start()
        out.wait()
        tops = [row_box[it, q, 0:blocks, :] for q in range(2)]
        top = jnp.maximum(tops[0], tops[1])
        total = sum(
            row_box[it, q, blocks : 2 * blocks, :] * jnp.exp2(tops[q] - top) for q in range(2)
        )
        f_all = math.log2(1.0 / live_total) - (top + jnp.log2(total))
        lane = lax.broadcasted_iota(jnp.int32, (1, BLOCK), 1)
        for t in range(blocks):
            live = lane < tiles_ref[2 * blocks + t]
            pot_train_ref[t : t + 1, :] = jnp.where(live, f_all[t : t + 1] * (1.0 / SCALE), 0.0)
            f = jnp.where(live, f_all[t : t + 1], FLOOR)
            for c in range(STRIPS):
                f_wide[pl.ds(t * BLOCK + c * LANES, LANES), :] = jnp.broadcast_to(
                    to_column(f[:, c * LANES : (c + 1) * LANES]), (LANES, LANES)
                )

        @pl.loop(0, blocks)
        def _(t):
            for k in range(2):
                for c in range(STRIPS):
                    score = f_wide[block_rows(t), :] - cost[t * 2 + k, :, strip(c)]
                    top = jnp.max(score, axis=0, keepdims=True)
                    total = jnp.sum(jnp.exp2(score - top), axis=0, keepdims=True)
                    tile_top[t * 2 + k, :, strip(c)] = top
                    tile_sum[t * 2 + k, :, strip(c)] = total

        for v in range(vals):
            top = jnp.full((1, BLOCK), FLOOR, jnp.float32)
            for q in range(2 * blocks):
                top = jnp.maximum(top, jnp.where(tiles_ref[q] == v, tile_top[q], FLOOR))
            total = jnp.zeros((1, BLOCK), jnp.float32)
            for q in range(2 * blocks):
                scaled = tile_sum[q] * jnp.exp2(jnp.minimum(tile_top[q] - top, 0.0))
                total = total + jnp.where(tiles_ref[q] == v, scaled, 0.0)
            val_box[it, me, v : v + 1, :] = top
            val_box[it, me, vals + v : vals + v + 1, :] = total

        @pl.loop(1, n)
        def _(d):
            val_copy(it, lax.rem(me + d, n), me).start()

        @pl.loop(1, n)
        def _(d):
            val_copy(it, lax.rem(me + d, n), lax.rem(me + d, n)).wait_recv()

        top = val_box[it, 0, 0:vals, :]
        for q in range(1, n):
            top = jnp.maximum(top, val_box[it, q, 0:vals, :])
        total = jnp.zeros((vals, BLOCK), jnp.float32)
        for q in range(n):
            total = total + val_box[it, q, vals : 2 * vals, :] * jnp.exp2(val_box[it, q, 0:vals, :] - top)
        g = math.log2(1.0 / val_total) - (top + jnp.log2(total))
        pot_val_ref[...] = g * (1.0 / SCALE)
        for v in range(vals):
            g_ref[v] = g[v : v + 1]

    @pl.loop(0, blocks)
    def _(t):
        g = [g_of(t * 2 + k) for k in range(2)]
        for c in range(STRIPS):
            f = f_wide[pl.ds(pl.multiple_of(t * BLOCK + c * LANES, LANES), LANES), :]
            total = jnp.zeros((LANES, LANES), jnp.float32)
            for k in range(2):
                for j in range(STRIPS):
                    value = jnp.exp2(
                        f + g[k][:, j * LANES : (j + 1) * LANES] - cost[t * 2 + k, strip(c), strip(j)]
                    )
                    total = total + value
                    plan[t * 2 + k, strip(c), strip(j)] = value.astype(jnp.bfloat16)
            mass_wide[pl.ds(pl.multiple_of(t * BLOCK + c * LANES, LANES), LANES), :] = (
                jnp.broadcast_to(jnp.sum(total, axis=1, keepdims=True), (LANES, LANES))
            )

    piece = share // PIECES

    def rows_of(j):
        return pl.ds(pl.multiple_of(j * piece, piece), piece)

    def pair_copy(s, j):
        return pltpu.make_async_remote_copy(
            src_ref=away.at[s, rows_of(j)], dst_ref=paired.at[s, rows_of(j)],
            send_sem=pair_send.at[s, j], recv_sem=pair_recv.at[s, j],
            device_id={"rows": mate}, device_id_type=MESH,
        )

    def own_copy(s, slot, j):
        goal = lax.rem(stage + 1 + s, pairs)
        return pltpu.make_async_remote_copy(
            src_ref=home.at[s, rows_of(j)], dst_ref=landed.at[slot, rows_of(j)],
            send_sem=own_send.at[s, j], recv_sem=own_recv.at[slot, j],
            device_id={"rows": goal * 2 + side}, device_id_type=MESH,
        )

    def merge_piece(s, j):
        pair_copy(s, j).wait_recv()
        home[s, rows_of(j)] = home[s, rows_of(j)] + paired[s, rows_of(j)]

    def relay(s):
        @pl.loop(0, PIECES)
        def _(j):
            merge_piece(s, j)
            own_copy(s, stage, j).start()

    def term_copy(t):
        return pltpu.make_async_remote_copy(
            src_ref=term_out.at[t], dst_ref=term_in.at[t],
            send_sem=term_send.at[t], recv_sem=term_recv.at[t],
            device_id={"cols": other}, device_id_type=MESH,
        )

    @pl.loop(0, pairs)
    def _(s):
        goal = lax.rem(stage + 1 + s, pairs)

        def push(which):
            start = (goal * 2 + which) * share
            v = lax.div(start, BLOCK)
            inside = lax.rem(start, BLOCK)
            total = jnp.zeros((share, width), jnp.float32)
            for t in range(blocks):
                if share % LANES == 0:
                    span = pl.ds(pl.multiple_of(inside, share), share)
                    parts = [plan[t * 2 + k, :, span] for k in range(2)]
                    offset = None
                else:
                    base = lax.div(inside, LANES) * LANES
                    span = pl.ds(pl.multiple_of(base, LANES), LANES)
                    parts = [plan[t * 2 + k, :, span] for k in range(2)]
                    offset = inside - base
                zero = jnp.zeros_like(parts[0])
                picked = jnp.where(
                    tiles_ref[t * 2][:, 0 : zero.shape[1]] == v, parts[0],
                    jnp.where(tiles_ref[t * 2 + 1][:, 0 : zero.shape[1]] == v, parts[1], zero),
                )
                product = lax.dot_general(
                    picked, x_ref[t * BLOCK : (t + 1) * BLOCK, :], (((0,), (0,)), ((), ())),
                    preferred_element_type=jnp.float32,
                )
                if offset is not None:
                    keep = product[0:share]
                    for piece in range(1, LANES // share):
                        keep = jnp.where(
                            offset == piece * share, product[piece * share : (piece + 1) * share], keep
                        )
                    product = keep
                total = total + product
            return total

        away[s] = push(1 - side)

        @pl.loop(0, PIECES)
        def _(j):
            pair_copy(s, j).start()

        home[s] = push(side)

    relay(0)

    @pl.loop(0, blocks)
    def _(t):
        mass = mass_wide[block_rows(t), 0:1]

        def pull(which):
            span = pl.ds(pl.multiple_of(which * half_width, LANES), half_width)
            total = mass * x_ref[block_rows(t), span].astype(jnp.float32)
            pulled = sum(
                jnp.dot(
                    plan[t * 2 + k], chosen[t * 2 + k, :, span],
                    preferred_element_type=jnp.float32,
                )
                for k in range(2)
            )
            return total - pulled

        term_out[t] = pull(other)
        term_copy(t).start()
        cost[t, :, 0:half_width] = pull(core)

    @pl.loop(1, pairs - 1)
    def _(s):
        relay(s)

    @pl.loop(0, blocks)
    def _(t):
        term_copy(t).wait()
        grad_train_ref[block_rows(t), :] = (
            live_total * 2.0 * (cost[t, :, 0:half_width] + term_in[t])
        ).astype(jnp.bfloat16)

    @pl.loop(0, PIECES)
    def _(j):
        merge_piece(pairs - 1, j)

    @pl.loop(0, pairs - 1)
    def _(s):
        slot = lax.rem(stage + 1 + s, pairs)

        @pl.loop(0, PIECES)
        def _(j):
            own_copy(s, slot, j).wait_recv()

        home[pairs - 1] = home[pairs - 1] + landed[slot]

    own_rows = y_ref[pl.ds(pl.multiple_of(me * share, share), share), :].astype(jnp.float32)
    grad_val_ref[...] = 2.0 * (own_rows - val_total * home[pairs - 1])

    @pl.loop(0, PIECES)
    def _(j):
        @pl.loop(0, pairs)
        def _(s):
            pair_copy(s, j).wait_send()

        @pl.loop(0, pairs - 1)
        def _(s):
            own_copy(s, stage, j).wait_send()

    @pl.loop(0, ITERS)
    def _(it):
        @pl.loop(1, n)
        def _(d):
            val_copy(it, lax.rem(me + d, n), me).wait_send()


def body(train_emb, val_emb, tiles, counts):
    n = lax.axis_size("rows")
    rows, width = train_emb.shape
    blocks = counts.shape[0]
    val_rows = val_emb.shape[1]
    vals = val_rows // BLOCK
    share = val_rows // n
    pairs = n // 2
    half = width // 2
    f32, bf16 = jnp.float32, jnp.bfloat16
    dma = pltpu.SemaphoreType.DMA
    vmem = pl.BlockSpec(memory_space=pltpu.VMEM)
    small = jnp.concatenate([tiles.reshape(-1), counts])
    pot_train, pot_val, grad_train, grad_val = pl.pallas_call(
        functools.partial(kernel, n, blocks, vals),
        out_shape=(
            jax.ShapeDtypeStruct((blocks, BLOCK), f32),
            jax.ShapeDtypeStruct((vals, BLOCK), f32),
            jax.ShapeDtypeStruct((rows, half), bf16),
            jax.ShapeDtypeStruct((share, width), f32),
        ),
        in_specs=[vmem, vmem, vmem],
        out_specs=(vmem, vmem, vmem, vmem),
        scratch_shapes=[
            pltpu.VMEM((2 * blocks, BLOCK, BLOCK), f32),
            pltpu.VMEM((2 * blocks, BLOCK, BLOCK), bf16),
            pltpu.VMEM((2 * blocks, BLOCK, width), bf16),
            pltpu.VMEM((vals, 1, BLOCK), f32),
            pltpu.VMEM((vals, 1, BLOCK), f32),
            pltpu.VMEM((rows, LANES), f32),
            pltpu.VMEM((rows, LANES), f32),
            pltpu.VMEM((2 * blocks, 1, BLOCK), f32),
            pltpu.VMEM((2 * blocks, 1, BLOCK), f32),
            pltpu.VMEM((2 * blocks, 1, BLOCK), f32),
            pltpu.VMEM((ITERS, 2, 2 * blocks, BLOCK), f32),
            pltpu.VMEM((ITERS, n, 2 * vals, BLOCK), f32),
            pltpu.VMEM((pairs, share, width), f32),
            pltpu.VMEM((pairs, share, width), f32),
            pltpu.VMEM((pairs, share, width), f32),
            pltpu.VMEM((pairs, share, width), f32),
            pltpu.VMEM((blocks, BLOCK, half), f32),
            pltpu.VMEM((blocks, BLOCK, half), f32),
            dma((ITERS,)), dma((ITERS,)),
            dma((ITERS, n)), dma((ITERS, n)),
            dma((pairs, PIECES)), dma((pairs, PIECES)),
            dma((pairs, PIECES)), dma((pairs, PIECES)),
            dma((blocks,)), dma((blocks,)),
        ],
        compiler_params=pltpu.CompilerParams(
            collective_id=0, has_side_effects=True, vmem_limit_bytes=56 * 1024 * 1024
        ),
    )(
        jnp.broadcast_to(small.reshape(-1, 1, 1), (3 * blocks, 1, BLOCK)),
        train_emb, val_emb.reshape(val_rows, width),
    )
    return (pot_train.reshape(-1), pot_val.reshape(1, -1), grad_train, grad_val[None])


def solution(mesh):
    return jax.shard_map(
        body,
        mesh=mesh,
        in_specs=(
            P(("groups", "rows"), None),
            P(("groups", "cols"), None, None),
            P(("groups", "rows"), "cols", None),
            P(("groups", "rows")),
        ),
        out_specs=(
            P(("groups", "rows")),
            P(("groups", "cols"), None),
            P(("groups", "rows"), "cols"),
            P(("groups", "cols"), "rows", None),
        ),
        check_vma=False,
    )
```
